32 devices in a mesh: vel: 8 (over z, y), space: 4 (over x, core).
Axes of the slice: x: 2, y: 2, z: 4, core: 2. Of those that a mesh axis runs over, the one named last changes fastest.
Arguments:
- initial: float32 [13824, 16, 128], P('vel', 'space'), as said below
- site_kind: int32 [16, 128], P('space'), may hold values from 0 to 2, as said below
Outputs:
- distribution: float32 [13824, 16, 128], P('vel', 'space')
- kelvin_level: float32 [16, 128], P('space')
The draws below stay inside these ranges and needn't reach their ends.
Inputs may be any that keep to these rules, and one draw needn't show every extreme that they name: `site_kind`: 0 marks a gas cell, 1 a wall cell, 2 an inflow cell. `initial`: every entry is positive.
All inputs are finite; a program needn't handle non-finite values.
Results may differ from the reference program's by a relative error of at most 0.0003.
Values sent between devices are 32-bit elements; how exact they have to be, the bound alone decides.
A program may use at most 64 MiB of HBM per device.

```python
import math
import jax
import jax.numpy as jnp
from jax import lax

NVX = 24
NODES_LATTICE = 13824
GRID_ROWS_Y = 128
STEPS = 2
GRID_ROWS_X = 16


def draw_initial(key, part):
    stochastic_seed_list = jax.random.split(key, 6)
    index = jnp.arange(NODES_LATTICE, dtype=jnp.int32)
    spacing = 8.0 / (NVX - 1)
    along_x_part = (-4.0 + spacing * (index // (NVX * NVX)).astype(jnp.float32))[:, None, None]
    along_y_part = (-4.0 + spacing * (index // NVX % NVX).astype(jnp.float32))[:, None, None]
    along_z_part = (-4.0 + spacing * (index % NVX).astype(jnp.float32))[:, None, None]
    particle_concentration = jnp.exp(jax.random.uniform(stochastic_seed_list[0], (GRID_ROWS_X, GRID_ROWS_Y), minval=math.log(0.4), maxval=math.log(2.5)))
    drift_range = 0.6
    jitter_low = 0.6
    jitter_high = 1.4
    average_drift_x = jax.random.uniform(stochastic_seed_list[1], (GRID_ROWS_X, GRID_ROWS_Y), minval=-drift_range, maxval=drift_range)
    average_drift_y = jax.random.uniform(stochastic_seed_list[2], (GRID_ROWS_X, GRID_ROWS_Y), minval=-drift_range, maxval=drift_range)
    average_drift_z = jax.random.uniform(stochastic_seed_list[3], (GRID_ROWS_X, GRID_ROWS_Y), minval=-drift_range, maxval=drift_range)
    kelvin_level = jnp.exp(jax.random.uniform(stochastic_seed_list[4], (GRID_ROWS_X, GRID_ROWS_Y), minval=math.log(0.6), maxval=math.log(1.8)))
    kinetic_variance = (along_x_part - average_drift_x[None]) ** 2 + (along_y_part - average_drift_y[None]) ** 2 + (along_z_part - average_drift_z[None]) ** 2
    gaussian_local_balance = particle_concentration[None] * kelvin_level[None] ** (-1.5) * jnp.exp(-kinetic_variance / (2.0 * kelvin_level[None]))
    jitter = jax.random.uniform(stochastic_seed_list[5], (NODES_LATTICE, GRID_ROWS_X, GRID_ROWS_Y), minval=jitter_low, maxval=jitter_high)
    return (gaussian_local_balance * jitter).astype(jnp.float32)


def draw_site_kind(key, part):
    levels = jax.random.randint(key, (GRID_ROWS_X, GRID_ROWS_Y), 0, 10)
    kind_labels = jnp.where(levels < 8, 0, jnp.where(levels < 9, 1, 2)).astype(jnp.int32)
    return kind_labels.at[0, 0].set(1).at[0, 1].set(2)


def setup_inputs(seed: int = 0) -> dict:
    key_list = jax.random.split(jax.random.key(seed), 3)
    initial = draw_initial(jax.random.fold_in(key_list[2], 71), 0)
    site_kind = draw_site_kind(jax.random.fold_in(key_list[2], 71), 0)
    return dict(initial=initial, site_kind=site_kind)


speed_limit = 4.0
courant = 0.1
diffusivity_ratio = 2.0 / 3.0
power_law_index = 0.81
encounter_rate = 0.25
wall_kelvin = 1.0
inflow_concentration = 1.0
inflow_speed = 0.5
inflow_kelvin = 1.0


def speeds(offset, amount):
    index = offset + jnp.arange(amount, dtype=jnp.int32)
    spacing = 2.0 * speed_limit / (NVX - 1)
    along_x_part = -speed_limit + spacing * (index // (NVX * NVX)).astype(jnp.float32)
    along_y_part = -speed_limit + spacing * ((index // NVX) % NVX).astype(jnp.float32)
    along_z_part = -speed_limit + spacing * (index % NVX).astype(jnp.float32)
    return along_x_part, along_y_part, along_z_part


def quad_weight():
    return (2.0 * speed_limit / (NVX - 1)) ** 3 / (2.0 * math.pi) ** 1.5


def minmod(left, right):
    return 0.5 * (jnp.sign(left) + jnp.sign(right)) * jnp.minimum(jnp.abs(left), jnp.abs(right))


def sweep(distribution_table, number, along):
    length = distribution_table.shape[along]

    def piece(source, low, high):
        return lax.slice_in_dim(source, low, high, axis=along)

    jumps = piece(distribution_table, 1, length) - piece(distribution_table, 0, length - 1)
    slopes = minmod(piece(jumps, 0, length - 2), piece(jumps, 1, length - 1))
    left_face = piece(distribution_table, 1, length - 2) + 0.5 * (1.0 - number) * piece(slopes, 0, length - 3)
    right_face = piece(distribution_table, 2, length - 1) - 0.5 * (1.0 + number) * piece(slopes, 1, length - 2)
    flux = number * jnp.where(number > 0, left_face, right_face)
    return piece(distribution_table, 2, length - 2) - (piece(flux, 1, length - 3) - piece(flux, 0, length - 4))


def transport(padded, along_x_part, along_y_part):
    swept = sweep(padded, courant * along_x_part[:, None, None], 1)
    widened = jnp.pad(swept, ((0, 0), (0, 0), (2, 2)))
    return sweep(widened, courant * along_y_part[:, None, None], 2)


def raw_table(along_x_part, along_y_part, along_z_part):
    magnitude_squares = along_x_part * along_x_part + along_y_part * along_y_part + along_z_part * along_z_part
    return quad_weight() * jnp.stack([jnp.ones_like(along_x_part), along_x_part, along_y_part, along_z_part, magnitude_squares])


def flow_drift_vector(integral_totals):
    particle_concentration = integral_totals[0]
    average_drift_x = integral_totals[1] / particle_concentration
    average_drift_y = integral_totals[2] / particle_concentration
    average_drift_z = integral_totals[3] / particle_concentration
    kelvin_level = (integral_totals[4] / particle_concentration - (average_drift_x * average_drift_x + average_drift_y * average_drift_y + average_drift_z * average_drift_z)) / 3.0
    return particle_concentration, average_drift_x, average_drift_y, average_drift_z, kelvin_level


def heat_terms(advected_distribution, along_x_part, along_y_part, along_z_part, average_drift_x, average_drift_y, average_drift_z):
    rel_x = along_x_part[:, None, None] - average_drift_x[None]
    rel_y = along_y_part[:, None, None] - average_drift_y[None]
    rel_z = along_z_part[:, None, None] - average_drift_z[None]
    scaled = 0.5 * quad_weight() * (rel_x * rel_x + rel_y * rel_y + rel_z * rel_z) * advected_distribution
    return jnp.stack([jnp.sum(rel_x * scaled, axis=0), jnp.sum(rel_y * scaled, axis=0), jnp.sum(rel_z * scaled, axis=0)])


def perform_relaxing(advected_distribution, kind_labels, along_x_part, along_y_part, along_z_part, particle_concentration, average_drift_x, average_drift_y, average_drift_z, kelvin_level, conductive_transfer):
    rel_x = along_x_part[:, None, None] - average_drift_x[None]
    rel_y = along_y_part[:, None, None] - average_drift_y[None]
    rel_z = along_z_part[:, None, None] - average_drift_z[None]
    relative_magnitude_square = rel_x * rel_x + rel_y * rel_y + rel_z * rel_z
    stress_scalar_grid = particle_concentration * kelvin_level
    gaussian_local_balance = particle_concentration * kelvin_level ** -1.5 * jnp.exp(-relative_magnitude_square / (2.0 * kelvin_level))
    conductive_vector_slot = rel_x * conductive_transfer[0] + rel_y * conductive_transfer[1] + rel_z * conductive_transfer[2]
    corrected_goal_distribution = gaussian_local_balance * (1.0 + (1.0 - diffusivity_ratio) * conductive_vector_slot * (relative_magnitude_square / kelvin_level - 5.0) / (5.0 * stress_scalar_grid * kelvin_level))
    approach_rate = encounter_rate * particle_concentration * kelvin_level ** (1.0 - power_law_index)
    relaxed = advected_distribution + approach_rate * (corrected_goal_distribution - advected_distribution)
    magnitude_squares = (along_x_part * along_x_part + along_y_part * along_y_part + along_z_part * along_z_part)[:, None, None]
    wall_distribution = particle_concentration * wall_kelvin ** -1.5 * jnp.exp(-magnitude_squares / (2.0 * wall_kelvin))
    inflow_magnitude_square = ((along_x_part - inflow_speed) ** 2 + along_y_part * along_y_part + along_z_part * along_z_part)[:, None, None]
    inflow_distribution = inflow_concentration * inflow_kelvin ** -1.5 * jnp.exp(-inflow_magnitude_square / (2.0 * inflow_kelvin))
    return jnp.where(kind_labels == 1, wall_distribution, jnp.where(kind_labels == 2, inflow_distribution, relaxed))


def reference(initial, site_kind):
    block = NVX * NVX
    distribution_table = initial.reshape(NVX, block, GRID_ROWS_X, GRID_ROWS_Y)
    starts = jnp.arange(NVX, dtype=jnp.int32) * block
    kelvin_level = jnp.zeros((GRID_ROWS_X, GRID_ROWS_Y), jnp.float32)
    for section in range(STEPS):
        def move_block(inputs):
            tile_elements, offset = inputs
            along_x_part, along_y_part, along_z_part = speeds(offset, block)
            padded = jnp.pad(tile_elements, ((0, 0), (2, 2), (0, 0)))
            advected_distribution = transport(padded, along_x_part, along_y_part)
            cumulative_total = jnp.einsum("kv,vrc->krc", raw_table(along_x_part, along_y_part, along_z_part), advected_distribution, precision=lax.Precision.HIGHEST)
            return advected_distribution, cumulative_total

        advected_distribution, cumulative_total = lax.map(move_block, (distribution_table, starts))
        particle_concentration, average_drift_x, average_drift_y, average_drift_z, kelvin_level = flow_drift_vector(jnp.sum(cumulative_total, axis=0))

        def heat_block(inputs):
            tile_elements, offset = inputs
            along_x_part, along_y_part, along_z_part = speeds(offset, block)
            return heat_terms(tile_elements, along_x_part, along_y_part, along_z_part, average_drift_x, average_drift_y, average_drift_z)

        conductive_transfer = jnp.sum(lax.map(heat_block, (advected_distribution, starts)), axis=0)

        def collide_block(inputs):
            tile_elements, offset = inputs
            along_x_part, along_y_part, along_z_part = speeds(offset, block)
            return perform_relaxing(tile_elements, site_kind, along_x_part, along_y_part, along_z_part, particle_concentration, average_drift_x, average_drift_y, average_drift_z, kelvin_level, conductive_transfer)

        distribution_table = lax.map(collide_block, (advected_distribution, starts))
    return distribution_table.reshape(NODES_LATTICE, GRID_ROWS_X, GRID_ROWS_Y), kelvin_level
```

```python
import functools
import math

import jax
import jax.numpy as jnp
from jax import lax
from jax.experimental import pallas as pl
from jax.experimental.pallas import tpu as pltpu
from jax.sharding import PartitionSpec as P

NVX = 24
HALF = NVX // 2
CHUNK = HALF * NVX
STEPS = 2
LIMIT = 4.0
COURANT = 0.1
SPACING = 2.0 * LIMIT / (NVX - 1)
WEIGHT = SPACING**3 / (2.0 * math.pi) ** 1.5
MESH = pl.DeviceIdType.MESH
LANES = 128
UNROLL = 2


def median0(p, r):
    return jnp.maximum(jnp.minimum(p, r), jnp.minimum(jnp.maximum(p, r), 0.0))


def sweep_rows(g, c, ck):
    d = [g[k + 1] - g[k] for k in range(6)]
    t = [ck * median0(d[k - 1], d[k]) for k in range(1, 6)]
    return [(g[k] - c * d[k - 1]) - (t[k - 1] - t[k - 2]) for k in range(2, 6)]


def sweep_lanes(f, c, ck, up_shift, down_shift, up_edge, down_edge):
    after = jnp.where(down_edge, 0.0, pltpu.roll(f, down_shift, 1))
    d = after - f
    before = jnp.where(up_edge, f, pltpu.roll(d, up_shift, 1))
    flux = c * f + ck * median0(before, d)
    return f - (flux - jnp.where(up_edge, 0.0, pltpu.roll(flux, up_shift, 1)))


def cell_parameters(total, kind):
    m = [total[k : k + 1] * WEIGHT for k in range(13)]
    rho = m[0]
    u = [m[1] / rho, m[2] / rho, m[3] / rho]
    energy = m[4] + m[5] + m[6]
    uu = u[0] * u[0] + u[1] * u[1] + u[2] * u[2]
    level = (energy / rho - uu) / 3.0
    um = u[0] * m[1] + u[1] * m[2] + u[2] * m[3]
    tail = energy - 2.0 * um + uu * rho
    second = [(4, 7, 8), (7, 5, 9), (8, 9, 6)]
    heat = []
    for i in range(3):
        mixed = sum(u[j] * m[second[i][j]] for j in range(3))
        heat.append(0.5 * (m[10 + i] - 2.0 * mixed + uu * m[1 + i] - u[i] * tail))
    inverse = 1.0 / level
    rate = 0.25 * rho * jnp.exp((1.0 - 0.81) * jnp.log(level))
    factor = rate * rho * inverse * lax.rsqrt(level)
    coupling = (1.0 - 2.0 / 3.0) / (5.0 * rho * level * level)
    gas = kind == 0
    wall = kind == 1
    zero = jnp.zeros_like(rho)
    rows = [
        jnp.where(gas, u[0], jnp.where(wall, 0.0, 0.5)),
        jnp.where(gas, u[1], 0.0),
        jnp.where(gas, u[2], 0.0),
        jnp.where(gas, inverse, 1.0),
        jnp.where(gas, coupling * heat[0], 0.0),
        jnp.where(gas, coupling * heat[1], 0.0),
        jnp.where(gas, coupling * heat[2], 0.0),
        jnp.where(gas, factor, jnp.where(wall, rho, 1.0)),
        jnp.where(gas, 1.0 - rate, 0.0),
        level,
    ]
    return jnp.concatenate(rows + [zero] * 6, axis=0)


def kernel(
    nv, ns, nchunk,
    x_ref, kind_ref, out_ref, level_ref,
    stage, first, second, third, halo1, halo2,
    acc, mom, gathered, par, near, tab_e, tab_o, tab_b,
    in_sem, out_sem, hs_down, hr_up, hs_up, hr_down,
    rs_send, rs_recv, ag_send, ag_recv, np_send, np_recv,
):
    me_v = lax.axis_index("vel")
    me_s = lax.axis_index("space")
    group = nv // 4
    positive = jnp.where(me_v >= nv // 2, 1, 0)
    sign = 2 * positive - 1
    down = me_s + sign
    up = me_s - sign
    has_down = jnp.logical_and(down >= 0, down < ns)
    has_up = jnp.logical_and(up >= 0, up < ns)
    down = jnp.clip(down, 0, ns - 1)
    up = jnp.clip(up, 0, ns - 1)
    halos = (halo1, halo2)

    def row_of(j):
        return j * sign + 3 * (1 - positive)

    def load_in(i):
        rows = pl.ds(pl.multiple_of(i * 4 * CHUNK, 4 * CHUNK), 4 * CHUNK)
        return pltpu.make_async_copy(x_ref.at[rows], stage.at[rows], in_sem.at[i])

    def store_out(i):
        rows = pl.ds(pl.multiple_of(i * 4 * CHUNK, 4 * CHUNK), 4 * CHUNK)
        return pltpu.make_async_copy(stage.at[rows], out_ref.at[rows], out_sem.at[i])

    def halo_down(step, src, i):
        rows = pl.ds(pl.multiple_of(i * CHUNK, CHUNK), CHUNK)
        return pltpu.make_async_remote_copy(
            src_ref=src.at[pl.ds(2, 2), rows], dst_ref=halos[step].at[pl.ds(0, 2), rows],
            send_sem=hs_down.at[step, i], recv_sem=hr_up.at[step, i],
            device_id={"space": down}, device_id_type=MESH)

    def halo_up(step, src, i):
        rows = pl.ds(pl.multiple_of(i * CHUNK, CHUNK), CHUNK)
        return pltpu.make_async_remote_copy(
            src_ref=src.at[pl.ds(0, 1), rows], dst_ref=halos[step].at[pl.ds(2, 1), rows],
            send_sem=hs_up.at[step, i], recv_sem=hr_down.at[step, i],
            device_id={"space": up}, device_id_type=MESH)

    def send_halo(step, src, i):
        @pl.when(has_down)
        def _():
            halo_down(step, src, i).start()

        @pl.when(has_up)
        def _():
            halo_up(step, src, i).start()

    def wait_halo(step, src, i):
        @pl.when(has_up)
        def _():
            halo_down(step, src, i).wait_recv()

        @pl.when(has_down)
        def _():
            halo_up(step, src, i).wait_recv()

    def wait_sent(step, src, i):
        @pl.when(has_down)
        def _():
            halo_down(step, src, i).wait_send()

        @pl.when(has_up)
        def _():
            halo_up(step, src, i).wait_send()

    pl.loop(0, nchunk)(lambda i: load_in(i).start())

    barrier = pltpu.get_barrier_semaphore()
    for k in range(1, nv):
        pl.semaphore_signal(barrier, inc=1, device_id={"vel": lax.rem(me_v + k, nv)}, device_id_type=MESH)

    @pl.when(has_down)
    def _():
        pl.semaphore_signal(barrier, inc=1, device_id={"space": down}, device_id_type=MESH)

    @pl.when(has_up)
    def _():
        pl.semaphore_signal(barrier, inc=1, device_id={"space": up}, device_id_type=MESH)

    @pl.when(jnp.logical_not(has_up))
    def _():
        def fill(i):
            for halo in halos:
                for n in range(2):
                    halo[n, pl.ds(pl.multiple_of(i * 32, 32), 32), :] = jnp.zeros((32, LANES), jnp.float32)
        pl.loop(0, nchunk * CHUNK // 32)(fill)
        near[0] = jnp.zeros((16, LANES), jnp.float32)
        near[1] = jnp.zeros((16, LANES), jnp.float32)

    @pl.when(jnp.logical_not(has_down))
    def _():
        def fill(i):
            for halo in halos:
                halo[2, pl.ds(pl.multiple_of(i * 32, 32), 32), :] = jnp.zeros((32, LANES), jnp.float32)
        pl.loop(0, nchunk * CHUNK // 32)(fill)
        near[2] = jnp.zeros((16, LANES), jnp.float32)

    pl.semaphore_wait(barrier, nv - 1 + jnp.where(has_down, 1, 0) + jnp.where(has_up, 1, 0))

    def spread(i):
        load_in(i).wait()

        def tile(n):
            for m in range(4):
                v = pl.multiple_of(i * CHUNK + n * 32, 32) + 8 * m
                for j in range(4):
                    first[j, pl.ds(v, 8), :] = stage[pl.ds(v * 4 + row_of(j), 8, stride=4), :]
        pl.loop(0, CHUNK // 32)(tile)
        send_halo(0, first, i)
    pl.loop(0, nchunk)(spread)

    sub = lax.broadcasted_iota(jnp.int32, (8, LANES), 0)
    lane = lax.broadcasted_iota(jnp.int32, (8, LANES), 1)

    def clear():
        for k in range(13):
            for j in range(4):
                acc[k, j] = jnp.zeros((8, LANES), jnp.float32)

    def speed(index):
        return -LIMIT + SPACING * index.astype(jnp.float32)

    def move(i, src, halo, dst, collided):
        chunk = me_v * nchunk + i
        half = lax.rem(chunk, 2)
        x1 = speed(chunk // 2)
        cx = COURANT * jnp.abs(x1)
        ckx = cx * 0.5 * (1.0 - cx)
        up_shift = jnp.where(half == 1, 1, LANES - 1)
        down_shift = LANES - up_shift
        up_lane = jnp.where(half == 1, 0, LANES - 1)
        up_edge = lane == up_lane
        down_edge = lane == LANES - 1 - up_lane
        base = i * CHUNK
        for e in range(NVX // 8):
            def one(b, sums):
                v = pl.ds(pl.multiple_of(base + b * NVX + 8 * e, 8), 8)
                x2 = speed(half * HALF + b)
                cy = COURANT * jnp.abs(x2)
                cky = cy * 0.5 * (1.0 - cy)
                g = [halo[0, v, :], halo[1, v, :]] + [src[j, v, :] for j in range(4)] + [halo[2, v, :]]
                if collided:
                    g = [collide(g[n], n, b, e) for n in range(7)]
                g = sweep_rows(g, cx, ckx)
                new = []
                for j in range(4):
                    o = sweep_lanes(g[j], cy, cky, up_shift, down_shift, up_edge, down_edge)
                    dst[j, v, :] = o
                    s0, s1, s2, s3 = sums[4 * j : 4 * j + 4]
                    o1 = x2 * o
                    o2 = x2 * o1
                    new += [s0 + o, s1 + o1, s2 + o2, s3 + x2 * o2]
                return tuple(new)

            def several(n, sums):
                for m in range(UNROLL):
                    sums = one(n * UNROLL + m, sums)
                return sums

            sums = lax.fori_loop(0, HALF // UNROLL, several, (jnp.zeros((8, LANES), jnp.float32),) * 16)
            x3 = speed(sub + 8 * e)
            for j in range(4):
                s0, s1, s2, s3 = sums[4 * j : 4 * j + 4]
                t1 = x1 * s0
                t3 = x3 * s0
                t11 = x1 * t1
                t33 = x3 * t3
                whole = t11 + s2 + t33
                terms = [s0, t1, s1, t3, t11, s2, t33, x1 * s1, x1 * t3, x3 * s1,
                         x1 * whole, (x1 * x1 + x3 * x3) * s1 + s3, x3 * whole]
                for k in range(13):
                    acc[k, j] = acc[k, j] + terms[k]

    def reduce(step):
        for j in range(4):
            rows = [jnp.sum(acc[k, j], axis=0, keepdims=True) for k in range(13)]
            mom[step, row_of(j)] = jnp.concatenate(rows + [jnp.zeros((3, LANES), jnp.float32)], axis=0)
        mine = me_v // group

        def part(k):
            to = lax.rem(me_v + k, nv)
            return pltpu.make_async_remote_copy(
                src_ref=mom.at[step, to // group], dst_ref=gathered.at[step, me_v],
                send_sem=rs_send.at[step, k], recv_sem=rs_recv.at[step, me_v],
                device_id={"vel": to}, device_id_type=MESH)

        def part_in(k):
            frm = lax.rem(me_v + k, nv)
            return pltpu.make_async_remote_copy(
                src_ref=mom.at[step, 0], dst_ref=gathered.at[step, frm],
                send_sem=rs_send.at[step, k], recv_sem=rs_recv.at[step, frm],
                device_id={"vel": frm}, device_id_type=MESH)

        for k in range(1, nv):
            part(k).start()
        gathered[step, me_v] = mom[step, mine]
        for k in range(1, nv):
            part_in(k).wait_recv()
        total = gathered[step, 0]
        for n in range(1, nv):
            total = total + gathered[step, n]
        par[step, mine] = cell_parameters(total, kind_ref[pl.ds(mine, 1), :])

        def share(k):
            to = lax.rem(mine + k, 4) * group + lax.rem(me_v, group)
            return pltpu.make_async_remote_copy(
                src_ref=par.at[step, mine], dst_ref=par.at[step, mine],
                send_sem=ag_send.at[step, k], recv_sem=ag_recv.at[step, mine],
                device_id={"vel": to}, device_id_type=MESH)

        def share_in(k):
            row = lax.rem(mine + k, 4)
            return pltpu.make_async_remote_copy(
                src_ref=par.at[step, mine], dst_ref=par.at[step, row],
                send_sem=ag_send.at[step, k], recv_sem=ag_recv.at[step, row],
                device_id={"vel": row * group + lax.rem(me_v, group)}, device_id_type=MESH)

        for k in range(1, 4):
            share(k).start()
        for k in range(1, 4):
            share_in(k).wait_recv()
        for k in range(1, nv):
            part(k).wait_send()
        for k in range(1, 4):
            share(k).wait_send()

    def near_copy(n):
        j, to = ((2, down), (3, down), (0, up))[n]
        return pltpu.make_async_remote_copy(
            src_ref=par.at[0, row_of(j)], dst_ref=near.at[n],
            send_sem=np_send.at[n], recv_sem=np_recv.at[n],
            device_id={"space": to}, device_id_type=MESH)

    def parameters(step, n):
        if n in (0, 1):
            return near[n]
        if n == 6:
            return near[2]
        return par[step, row_of(n - 2)]

    def build_e(step, rows):
        x3 = speed(lax.broadcasted_iota(jnp.int32, (NVX, LANES), 0))
        for n in rows:
            p = parameters(step, n)
            c3 = x3 - p[2:3]
            quad = c3 * c3 * p[3:4]
            tab_e[0, n] = quad
            tab_e[1, n] = p[6:7] * c3
            tab_e[2, n] = jnp.exp(-0.5 * quad)
            tab_o[n] = jnp.broadcast_to(p[8:9], (8, LANES))

    def build_b(step, i, rows):
        chunk = me_v * nchunk + i
        x1 = speed(chunk // 2)
        x2 = speed(lax.rem(chunk, 2) * HALF + lax.broadcasted_iota(jnp.int32, (16, LANES), 0))
        for n in rows:
            p = parameters(step, n)
            c1 = x1 - p[0:1]
            c2 = x2 - p[1:2]
            quad = (c1 * c1 + c2 * c2) * p[3:4]
            tab_b[0, n] = quad - 5.0
            tab_b[1, n] = p[4:5] * c1 + p[5:6] * c2
            tab_b[2, n] = p[7:8] * jnp.exp(-0.5 * quad)

    def collide(f, n, b, e):
        es = pl.ds(8 * e, 8)
        bs = pl.ds(b, 1)
        quad = tab_b[0, n, bs, :] + tab_e[0, n, es, :]
        flow = tab_b[1, n, bs, :] + tab_e[1, n, es, :]
        gauss = tab_b[2, n, bs, :] * tab_e[2, n, es, :]
        return tab_o[n] * f + gauss * (1.0 + flow * quad)

    clear()

    def step_one(i):
        wait_halo(0, first, i)
        move(i, first, halo1, second, False)
        send_halo(1, second, i)
    pl.loop(0, nchunk)(step_one)
    reduce(0)

    @pl.when(has_down)
    def _():
        near_copy(0).start()
        near_copy(1).start()

    @pl.when(has_up)
    def _():
        near_copy(2).start()
    clear()

    @pl.when(has_up)
    def _():
        near_copy(0).wait_recv()
        near_copy(1).wait_recv()

    @pl.when(has_down)
    def _():
        near_copy(2).wait_recv()

    build_e(0, range(7))

    def step_two(i):
        build_b(0, i, range(7))
        wait_halo(1, second, i)
        move(i, second, halo2, third, True)
    pl.loop(0, nchunk)(step_two)
    reduce(1)

    own = range(2, 6)
    build_e(1, own)

    def finish(i):
        build_b(1, i, own)
        for e in range(NVX // 8):
            def one(n):
                for m in range(UNROLL):
                    b = n * UNROLL + m
                    v = pl.multiple_of(i * CHUNK + b * NVX + 8 * e, 8)
                    for j in range(4):
                        stage[pl.ds(v * 4 + row_of(j), 8, stride=4), :] = collide(
                            third[j, pl.ds(v, 8), :], j + 2, b, e)
            pl.loop(0, HALF // UNROLL)(one)
        store_out(i).start()
    pl.loop(0, nchunk)(finish)

    for r in range(4):
        level_ref[r : r + 1, :] = par[1, r, 9:10, :]

    def drain(i):
        wait_sent(0, first, i)
        wait_sent(1, second, i)
        store_out(i).wait()
    pl.loop(0, nchunk)(drain)

    @pl.when(has_down)
    def _():
        near_copy(0).wait_send()
        near_copy(1).wait_send()

    @pl.when(has_up)
    def _():
        near_copy(2).wait_send()


def per_device(nv, ns, initial, site_kind):
    amount, rows, lanes = initial.shape
    assert rows == 4 and lanes == LANES and amount % CHUNK == 0
    assert nv % 4 == 0 and (NVX * NVX * HALF) % amount == 0
    nchunk = amount // CHUNK
    f32 = jnp.float32
    dma = pltpu.SemaphoreType.DMA
    out, level = pl.pallas_call(
        functools.partial(kernel, nv, ns, nchunk),
        out_shape=(
            jax.ShapeDtypeStruct((amount * 4, LANES), f32),
            jax.ShapeDtypeStruct((4, LANES), f32),
        ),
        in_specs=[pl.BlockSpec(memory_space=pl.ANY), pl.BlockSpec(memory_space=pltpu.VMEM)],
        out_specs=(pl.BlockSpec(memory_space=pl.ANY), pl.BlockSpec(memory_space=pltpu.VMEM)),
        scratch_shapes=[
            pltpu.VMEM((amount * 4, LANES), f32),
            pltpu.VMEM((4, amount, LANES), f32),
            pltpu.VMEM((4, amount, LANES), f32),
            pltpu.VMEM((4, amount, LANES), f32),
            pltpu.VMEM((3, amount, LANES), f32),
            pltpu.VMEM((3, amount, LANES), f32),
            pltpu.VMEM((13, 4, 8, LANES), f32),
            pltpu.VMEM((2, 4, 16, LANES), f32),
            pltpu.VMEM((2, nv, 16, LANES), f32),
            pltpu.VMEM((2, 4, 16, LANES), f32),
            pltpu.VMEM((3, 16, LANES), f32),
            pltpu.VMEM((3, 7, NVX, LANES), f32),
            pltpu.VMEM((7, 8, LANES), f32),
            pltpu.VMEM((3, 7, 16, LANES), f32),
            dma((nchunk,)), dma((nchunk,)),
            dma((2, nchunk)), dma((2, nchunk)), dma((2, nchunk)), dma((2, nchunk)),
            dma((2, nv)), dma((2, nv)), dma((2, 4)), dma((2, 4)), dma((3,)), dma((3,)),
        ],
        compiler_params=pltpu.CompilerParams(
            collective_id=0, has_side_effects=True, vmem_limit_bytes=40 * 1024 * 1024
        ),
    )(initial.reshape(amount * 4, LANES), site_kind)
    return out.reshape(amount, 4, LANES), level


def solution(mesh):
    return jax.shard_map(
        functools.partial(per_device, mesh.shape["vel"], mesh.shape["space"]),
        mesh=mesh,
        in_specs=(P("vel", "space", None), P("space", None)),
        out_specs=(P("vel", "space", None), P("space", None)),
        check_vma=False,
    )
```

```python
import functools
import math

import jax
import jax.numpy as jnp
from jax import lax
from jax.experimental import pallas as pl
from jax.experimental.pallas import tpu as pltpu
from jax.sharding import PartitionSpec as P

NVX = 24
HALF = NVX // 2
CHUNK = HALF * NVX
STEPS = 2
LIMIT = 4.0
COURANT = 0.1
SPACING = 2.0 * LIMIT / (NVX - 1)
WEIGHT = SPACING**3 / (2.0 * math.pi) ** 1.5
MESH = pl.DeviceIdType.MESH
LANES = 128
UNROLL = 6


def median0(p, r):
    return jnp.maximum(jnp.minimum(p, r), jnp.minimum(jnp.maximum(p, r), 0.0))


def sweep_rows(g, c, ck):
    d = [g[k + 1] - g[k] for k in range(6)]
    t = [ck * median0(d[k - 1], d[k]) for k in range(1, 6)]
    return [(g[k] - c * d[k - 1]) - (t[k - 1] - t[k - 2]) for k in range(2, 6)]


def sweep_lanes(f, c, ck, up_shift, down_shift, up_edge, down_edge):
    after = jnp.where(down_edge, 0.0, pltpu.roll(f, down_shift, 1))
    d = after - f
    before = jnp.where(up_edge, f, pltpu.roll(d, up_shift, 1))
    flux = c * f + ck * median0(before, d)
    return f - (flux - jnp.where(up_edge, 0.0, pltpu.roll(flux, up_shift, 1)))


def cell_parameters(total, kind):
    m = [total[k : k + 1] * WEIGHT for k in range(13)]
    rho = m[0]
    u = [m[1] / rho, m[2] / rho, m[3] / rho]
    energy = m[4] + m[5] + m[6]
    uu = u[0] * u[0] + u[1] * u[1] + u[2] * u[2]
    level = (energy / rho - uu) / 3.0
    um = u[0] * m[1] + u[1] * m[2] + u[2] * m[3]
    tail = energy - 2.0 * um + uu * rho
    second = [(4, 7, 8), (7, 5, 9), (8, 9, 6)]
    heat = []
    for i in range(3):
        mixed = sum(u[j] * m[second[i][j]] for j in range(3))
        heat.append(0.5 * (m[10 + i] - 2.0 * mixed + uu * m[1 + i] - u[i] * tail))
    inverse = 1.0 / level
    rate = 0.25 * rho * jnp.exp((1.0 - 0.81) * jnp.log(level))
    factor = rate * rho * inverse * lax.rsqrt(level)
    coupling = (1.0 - 2.0 / 3.0) / (5.0 * rho * level * level)
    gas = kind == 0
    wall = kind == 1
    zero = jnp.zeros_like(rho)
    rows = [
        jnp.where(gas, u[0], jnp.where(wall, 0.0, 0.5)),
        jnp.where(gas, u[1], 0.0),
        jnp.where(gas, u[2], 0.0),
        jnp.where(gas, inverse, 1.0),
        jnp.where(gas, coupling * heat[0], 0.0),
        jnp.where(gas, coupling * heat[1], 0.0),
        jnp.where(gas, coupling * heat[2], 0.0),
        jnp.where(gas, factor, jnp.where(wall, rho, 1.0)),
        jnp.where(gas, 1.0 - rate, 0.0),
        level,
    ]
    return jnp.concatenate(rows + [zero] * 6, axis=0)


def kernel(
    nv, ns, nchunk,
    x_ref, kind_ref, out_ref, level_ref,
    stage, first, second, third, halo1, halo2,
    acc, mom, gathered, par, near, tab_e, tab_o, tab_b,
    in_sem, out_sem, hs_down, hr_up, hs_up, hr_down,
    rs_send, rs_recv, ag_send, ag_recv, np_send, np_recv,
):
    me_v = lax.axis_index("vel")
    me_s = lax.axis_index("space")
    group = nv // 4
    positive = jnp.where(me_v >= nv // 2, 1, 0)
    sign = 2 * positive - 1
    down = me_s + sign
    up = me_s - sign
    has_down = jnp.logical_and(down >= 0, down < ns)
    has_up = jnp.logical_and(up >= 0, up < ns)
    down = jnp.clip(down, 0, ns - 1)
    up = jnp.clip(up, 0, ns - 1)
    halos = (halo1, halo2)
    early = nchunk // 2

    def row_of(j):
        return j * sign + 3 * (1 - positive)

    def load_in(i):
        rows = pl.ds(pl.multiple_of(i * 4 * CHUNK, 4 * CHUNK), 4 * CHUNK)
        return pltpu.make_async_copy(x_ref.at[rows], stage.at[rows], in_sem.at[i])

    def store_out(i):
        rows = pl.ds(pl.multiple_of(i * 4 * CHUNK, 4 * CHUNK), 4 * CHUNK)
        return pltpu.make_async_copy(stage.at[rows], out_ref.at[rows], out_sem.at[i])

    def halo_down(step, src, i):
        rows = pl.ds(pl.multiple_of(i * CHUNK, CHUNK), CHUNK)
        return pltpu.make_async_remote_copy(
            src_ref=src.at[pl.ds(2, 2), rows], dst_ref=halos[step].at[pl.ds(0, 2), rows],
            send_sem=hs_down.at[step, i], recv_sem=hr_up.at[step, i],
            device_id={"space": down}, device_id_type=MESH)

    def halo_up(step, src, i):
        rows = pl.ds(pl.multiple_of(i * CHUNK, CHUNK), CHUNK)
        return pltpu.make_async_remote_copy(
            src_ref=src.at[pl.ds(0, 1), rows], dst_ref=halos[step].at[pl.ds(2, 1), rows],
            send_sem=hs_up.at[step, i], recv_sem=hr_down.at[step, i],
            device_id={"space": up}, device_id_type=MESH)

    def send_halo(step, src, i):
        @pl.when(has_down)
        def _():
            halo_down(step, src, i).start()

        @pl.when(has_up)
        def _():
            halo_up(step, src, i).start()

    def wait_halo(step, src, i):
        @pl.when(has_up)
        def _():
            halo_down(step, src, i).wait_recv()

        @pl.when(has_down)
        def _():
            halo_up(step, src, i).wait_recv()

    def wait_sent(step, src, i):
        @pl.when(has_down)
        def _():
            halo_down(step, src, i).wait_send()

        @pl.when(has_up)
        def _():
            halo_up(step, src, i).wait_send()

    pl.loop(0, nchunk)(lambda i: load_in(i).start())

    barrier = pltpu.get_barrier_semaphore()
    for k in range(1, nv):
        pl.semaphore_signal(barrier, inc=1, device_id={"vel": lax.rem(me_v + k, nv)}, device_id_type=MESH)

    @pl.when(has_down)
    def _():
        pl.semaphore_signal(barrier, inc=1, device_id={"space": down}, device_id_type=MESH)

    @pl.when(has_up)
    def _():
        pl.semaphore_signal(barrier, inc=1, device_id={"space": up}, device_id_type=MESH)

    @pl.when(jnp.logical_not(has_up))
    def _():
        def fill(i):
            for halo in halos:
                for n in range(2):
                    halo[n, pl.ds(pl.multiple_of(i * 32, 32), 32), :] = jnp.zeros((32, LANES), jnp.float32)
        pl.loop(0, nchunk * CHUNK // 32)(fill)
        near[0] = jnp.zeros((16, LANES), jnp.float32)
        near[1] = jnp.zeros((16, LANES), jnp.float32)

    @pl.when(jnp.logical_not(has_down))
    def _():
        def fill(i):
            for halo in halos:
                halo[2, pl.ds(pl.multiple_of(i * 32, 32), 32), :] = jnp.zeros((32, LANES), jnp.float32)
        pl.loop(0, nchunk * CHUNK // 32)(fill)
        near[2] = jnp.zeros((16, LANES), jnp.float32)

    pl.semaphore_wait(barrier, nv - 1 + jnp.where(has_down, 1, 0) + jnp.where(has_up, 1, 0))

    def spread(i):
        load_in(i).wait()

        def tile(n):
            for m in range(4):
                v = pl.multiple_of(i * CHUNK + n * 32, 32) + 8 * m
                for j in range(4):
                    first[j, pl.ds(v, 8), :] = stage[pl.ds(v * 4 + row_of(j), 8, stride=4), :]
        pl.loop(0, CHUNK // 32)(tile)
        send_halo(0, first, i)
    pl.loop(0, nchunk)(spread)

    sub = lax.broadcasted_iota(jnp.int32, (8, LANES), 0)
    lane = lax.broadcasted_iota(jnp.int32, (8, LANES), 1)

    def clear():
        for k in range(13):
            for j in range(4):
                acc[k, j] = jnp.zeros((8, LANES), jnp.float32)

    def speed(index):
        return -LIMIT + SPACING * index.astype(jnp.float32)

    def move(i, src, halo, dst, collided):
        chunk = me_v * nchunk + i
        half = lax.rem(chunk, 2)
        x1 = speed(chunk // 2)
        cx = COURANT * jnp.abs(x1)
        ckx = cx * 0.5 * (1.0 - cx)
        up_shift = jnp.where(half == 1, 1, LANES - 1)
        down_shift = LANES - up_shift
        up_lane = jnp.where(half == 1, 0, LANES - 1)
        up_edge = lane == up_lane
        down_edge = lane == LANES - 1 - up_lane
        base = i * CHUNK
        for e in range(NVX // 8):
            def one(b, sums):
                v = pl.ds(pl.multiple_of(base + b * NVX + 8 * e, 8), 8)
                x2 = speed(half * HALF + b)
                cy = COURANT * jnp.abs(x2)
                cky = cy * 0.5 * (1.0 - cy)
                g = [halo[0, v, :], halo[1, v, :]] + [src[j, v, :] for j in range(4)] + [halo[2, v, :]]
                if collided:
                    g = [collide(g[n], n, b, e) for n in range(7)]
                g = sweep_rows(g, cx, ckx)
                new = []
                for j in range(4):
                    o = sweep_lanes(g[j], cy, cky, up_shift, down_shift, up_edge, down_edge)
                    dst[j, v, :] = o
                    s0, s1, s2, s3 = sums[4 * j : 4 * j + 4]
                    o1 = x2 * o
                    o2 = x2 * o1
                    new += [s0 + o, s1 + o1, s2 + o2, s3 + x2 * o2]
                return tuple(new)

            def several(n, sums):
                for m in range(UNROLL):
                    sums = one(n * UNROLL + m, sums)
                return sums

            sums = lax.fori_loop(0, HALF // UNROLL, several, (jnp.zeros((8, LANES), jnp.float32),) * 16)
            x3 = speed(sub + 8 * e)
            for j in range(4):
                s0, s1, s2, s3 = sums[4 * j : 4 * j + 4]
                t1 = x1 * s0
                t3 = x3 * s0
                t11 = x1 * t1
                t33 = x3 * t3
                whole = t11 + s2 + t33
                terms = [s0, t1, s1, t3, t11, s2, t33, x1 * s1, x1 * t3, x3 * s1,
                         x1 * whole, (x1 * x1 + x3 * x3) * s1 + s3, x3 * whole]
                for k in range(13):
                    acc[k, j] = acc[k, j] + terms[k]

    def reduce(step):
        for j in range(4):
            rows = [jnp.sum(acc[k, j], axis=0, keepdims=True) for k in range(13)]
            mom[step, row_of(j)] = jnp.concatenate(rows + [jnp.zeros((3, LANES), jnp.float32)], axis=0)
        mine = me_v // group

        def part(k):
            to = lax.rem(me_v + k, nv)
            return pltpu.make_async_remote_copy(
                src_ref=mom.at[step, to // group], dst_ref=gathered.at[step, me_v],
                send_sem=rs_send.at[step, k], recv_sem=rs_recv.at[step, me_v],
                device_id={"vel": to}, device_id_type=MESH)

        def part_in(k):
            frm = lax.rem(me_v + k, nv)
            return pltpu.make_async_remote_copy(
                src_ref=mom.at[step, 0], dst_ref=gathered.at[step, frm],
                send_sem=rs_send.at[step, k], recv_sem=rs_recv.at[step, frm],
                device_id={"vel": frm}, device_id_type=MESH)

        for k in range(1, nv):
            part(k).start()
        gathered[step, me_v] = mom[step, mine]
        for k in range(1, nv):
            part_in(k).wait_recv()
        total = gathered[step, 0]
        for n in range(1, nv):
            total = total + gathered[step, n]
        par[step, mine] = cell_parameters(total, kind_ref[pl.ds(mine, 1), :])

        def share(k):
            to = lax.rem(mine + k, 4) * group + lax.rem(me_v, group)
            return pltpu.make_async_remote_copy(
                src_ref=par.at[step, mine], dst_ref=par.at[step, mine],
                send_sem=ag_send.at[step, k], recv_sem=ag_recv.at[step, mine],
                device_id={"vel": to}, device_id_type=MESH)

        def share_in(k):
            row = lax.rem(mine + k, 4)
            return pltpu.make_async_remote_copy(
                src_ref=par.at[step, mine], dst_ref=par.at[step, row],
                send_sem=ag_send.at[step, k], recv_sem=ag_recv.at[step, row],
                device_id={"vel": row * group + lax.rem(me_v, group)}, device_id_type=MESH)

        for k in range(1, 4):
            share(k).start()
        for k in range(1, 4):
            share_in(k).wait_recv()
        for k in range(1, nv):
            part(k).wait_send()
        for k in range(1, 4):
            share(k).wait_send()

    def near_copy(n):
        j, to = ((2, down), (3, down), (0, up))[n]
        return pltpu.make_async_remote_copy(
            src_ref=par.at[0, row_of(j)], dst_ref=near.at[n],
            send_sem=np_send.at[n], recv_sem=np_recv.at[n],
            device_id={"space": to}, device_id_type=MESH)

    def parameters(step, n):
        if n in (0, 1):
            return near[n]
        if n == 6:
            return near[2]
        return par[step, row_of(n - 2)]

    def build_e(step, rows):
        x3 = speed(lax.broadcasted_iota(jnp.int32, (NVX, LANES), 0))
        for n in rows:
            p = parameters(step, n)
            c3 = x3 - p[2:3]
            quad = c3 * c3 * p[3:4]
            tab_e[0, n] = quad
            tab_e[1, n] = p[6:7] * c3
            tab_e[2, n] = jnp.exp(-0.5 * quad)
            tab_o[n] = jnp.broadcast_to(p[8:9], (8, LANES))

    def build_b(step, i, rows):
        chunk = me_v * nchunk + i
        x1 = speed(chunk // 2)
        x2 = speed(lax.rem(chunk, 2) * HALF + lax.broadcasted_iota(jnp.int32, (16, LANES), 0))
        for n in rows:
            p = parameters(step, n)
            c1 = x1 - p[0:1]
            c2 = x2 - p[1:2]
            quad = (c1 * c1 + c2 * c2) * p[3:4]
            tab_b[0, n] = quad - 5.0
            tab_b[1, n] = p[4:5] * c1 + p[5:6] * c2
            tab_b[2, n] = p[7:8] * jnp.exp(-0.5 * quad)

    def collide(f, n, b, e):
        es = pl.ds(8 * e, 8)
        bs = pl.ds(b, 1)
        quad = tab_b[0, n, bs, :] + tab_e[0, n, es, :]
        flow = tab_b[1, n, bs, :] + tab_e[1, n, es, :]
        gauss = tab_b[2, n, bs, :] * tab_e[2, n, es, :]
        return tab_o[n] * f + gauss * (1.0 + flow * quad)

    clear()

    def step_one(i):
        wait_halo(0, first, i)
        move(i, first, halo1, second, False)

        @pl.when(i < early)
        def _():
            send_halo(1, second, i)
    pl.loop(0, nchunk)(step_one)
    reduce(0)

    @pl.when(has_down)
    def _():
        near_copy(0).start()
        near_copy(1).start()

    @pl.when(has_up)
    def _():
        near_copy(2).start()
    pl.loop(early, nchunk)(lambda i: send_halo(1, second, i))
    clear()

    @pl.when(has_up)
    def _():
        near_copy(0).wait_recv()
        near_copy(1).wait_recv()

    @pl.when(has_down)
    def _():
        near_copy(2).wait_recv()

    build_e(0, range(7))

    def step_two(i):
        build_b(0, i, range(7))
        wait_halo(1, second, i)
        move(i, second, halo2, third, True)
    pl.loop(0, nchunk)(step_two)
    reduce(1)

    own = range(2, 6)
    build_e(1, own)

    def finish(i):
        build_b(1, i, own)
        for e in range(NVX // 8):
            def one(n):
                for m in range(UNROLL):
                    b = n * UNROLL + m
                    v = pl.multiple_of(i * CHUNK + b * NVX + 8 * e, 8)
                    for j in range(4):
                        stage[pl.ds(v * 4 + row_of(j), 8, stride=4), :] = collide(
                            third[j, pl.ds(v, 8), :], j + 2, b, e)
            pl.loop(0, HALF // UNROLL)(one)
        store_out(i).start()
    pl.loop(0, nchunk)(finish)

    for r in range(4):
        level_ref[r : r + 1, :] = par[1, r, 9:10, :]

    def drain(i):
        wait_sent(0, first, i)
        wait_sent(1, second, i)
        store_out(i).wait()
    pl.loop(0, nchunk)(drain)

    @pl.when(has_down)
    def _():
        near_copy(0).wait_send()
        near_copy(1).wait_send()

    @pl.when(has_up)
    def _():
        near_copy(2).wait_send()


def per_device(nv, ns, initial, site_kind):
    amount, rows, lanes = initial.shape
    assert rows == 4 and lanes == LANES and amount % CHUNK == 0
    assert nv % 4 == 0 and (NVX * NVX * HALF) % amount == 0
    nchunk = amount // CHUNK
    f32 = jnp.float32
    dma = pltpu.SemaphoreType.DMA
    out, level = pl.pallas_call(
        functools.partial(kernel, nv, ns, nchunk),
        out_shape=(
            jax.ShapeDtypeStruct((amount * 4, LANES), f32),
            jax.ShapeDtypeStruct((4, LANES), f32),
        ),
        in_specs=[pl.BlockSpec(memory_space=pl.ANY), pl.BlockSpec(memory_space=pltpu.VMEM)],
        out_specs=(pl.BlockSpec(memory_space=pl.ANY), pl.BlockSpec(memory_space=pltpu.VMEM)),
        scratch_shapes=[
            pltpu.VMEM((amount * 4, LANES), f32),
            pltpu.VMEM((4, amount, LANES), f32),
            pltpu.VMEM((4, amount, LANES), f32),
            pltpu.VMEM((4, amount, LANES), f32),
            pltpu.VMEM((3, amount, LANES), f32),
            pltpu.VMEM((3, amount, LANES), f32),
            pltpu.VMEM((13, 4, 8, LANES), f32),
            pltpu.VMEM((2, 4, 16, LANES), f32),
            pltpu.VMEM((2, nv, 16, LANES), f32),
            pltpu.VMEM((2, 4, 16, LANES), f32),
            pltpu.VMEM((3, 16, LANES), f32),
            pltpu.VMEM((3, 7, NVX, LANES), f32),
            pltpu.VMEM((7, 8, LANES), f32),
            pltpu.VMEM((3, 7, 16, LANES), f32),
            dma((nchunk,)), dma((nchunk,)),
            dma((2, nchunk)), dma((2, nchunk)), dma((2, nchunk)), dma((2, nchunk)),
            dma((2, nv)), dma((2, nv)), dma((2, 4)), dma((2, 4)), dma((3,)), dma((3,)),
        ],
        compiler_params=pltpu.CompilerParams(
            collective_id=0, has_side_effects=True, vmem_limit_bytes=40 * 1024 * 1024
        ),
    )(initial.reshape(amount * 4, LANES), site_kind)
    return out.reshape(amount, 4, LANES), level


def solution(mesh):
    return jax.shard_map(
        functools.partial(per_device, mesh.shape["vel"], mesh.shape["space"]),
        mesh=mesh,
        in_specs=(P("vel", "space", None), P("space", None)),
        out_specs=(P("vel", "space", None), P("space", None)),
        check_vma=False,
    )
```

```python
import functools
import math

import jax
import jax.numpy as jnp
from jax import lax
from jax.experimental import pallas as pl
from jax.experimental.pallas import tpu as pltpu
from jax.sharding import PartitionSpec as P

NVX = 24
HALF = NVX // 2
CHUNK = HALF * NVX
STEPS = 2
LIMIT = 4.0
COURANT = 0.1
SPACING = 2.0 * LIMIT / (NVX - 1)
WEIGHT = SPACING**3 / (2.0 * math.pi) ** 1.5
MESH = pl.DeviceIdType.MESH
LANES = 128
UNROLL = 6


def median0(p, r):
    return jnp.maximum(jnp.minimum(p, r), jnp.minimum(jnp.maximum(p, r), 0.0))


def sweep_rows(g, c, ck):
    d = [g[k + 1] - g[k] for k in range(6)]
    t = [ck * median0(d[k - 1], d[k]) for k in range(1, 6)]
    return [(g[k] - c * d[k - 1]) - (t[k - 1] - t[k - 2]) for k in range(2, 6)]


def sweep_lanes(f, c, ck, up_shift, down_shift, up_edge, down_edge):
    after = jnp.where(down_edge, 0.0, pltpu.roll(f, down_shift, 1))
    d = after - f
    before = jnp.where(up_edge, f, pltpu.roll(d, up_shift, 1))
    flux = c * f + ck * median0(before, d)
    return f - (flux - jnp.where(up_edge, 0.0, pltpu.roll(flux, up_shift, 1)))


def cell_parameters(total, kind):
    m = [total[k : k + 1] * WEIGHT for k in range(13)]
    rho = m[0]
    u = [m[1] / rho, m[2] / rho, m[3] / rho]
    energy = m[4] + m[5] + m[6]
    uu = u[0] * u[0] + u[1] * u[1] + u[2] * u[2]
    level = (energy / rho - uu) / 3.0
    um = u[0] * m[1] + u[1] * m[2] + u[2] * m[3]
    tail = energy - 2.0 * um + uu * rho
    second = [(4, 7, 8), (7, 5, 9), (8, 9, 6)]
    heat = []
    for i in range(3):
        mixed = sum(u[j] * m[second[i][j]] for j in range(3))
        heat.append(0.5 * (m[10 + i] - 2.0 * mixed + uu * m[1 + i] - u[i] * tail))
    inverse = 1.0 / level
    rate = 0.25 * rho * jnp.exp((1.0 - 0.81) * jnp.log(level))
    factor = rate * rho * inverse * lax.rsqrt(level)
    coupling = (1.0 - 2.0 / 3.0) / (5.0 * rho * level * level)
    gas = kind == 0
    wall = kind == 1
    zero = jnp.zeros_like(rho)
    rows = [
        jnp.where(gas, u[0], jnp.where(wall, 0.0, 0.5)),
        jnp.where(gas, u[1], 0.0),
        jnp.where(gas, u[2], 0.0),
        jnp.where(gas, inverse, 1.0),
        jnp.where(gas, coupling * heat[0], 0.0),
        jnp.where(gas, coupling * heat[1], 0.0),
        jnp.where(gas, coupling * heat[2], 0.0),
        jnp.where(gas, factor, jnp.where(wall, rho, 1.0)),
        jnp.where(gas, 1.0 - rate, 0.0),
        level,
    ]
    return jnp.concatenate(rows + [zero] * 6, axis=0)


def kernel(
    nv, ns, nchunk,
    x_ref, kind_ref, out_ref, level_ref,
    stage, first, second, third, halo1, halo2,
    acc, mom, gathered, par, near, tab_e, tab_o, tab_b,
    in_sem, hs_down, hr_up, hs_up, hr_down,
    rs_send, rs_recv, ag_send, ag_recv, np_send, np_recv,
):
    me_v = lax.axis_index("vel")
    me_s = lax.axis_index("space")
    group = nv // 4
    positive = jnp.where(me_v >= nv // 2, 1, 0)
    sign = 2 * positive - 1
    down = me_s + sign
    up = me_s - sign
    has_down = jnp.logical_and(down >= 0, down < ns)
    has_up = jnp.logical_and(up >= 0, up < ns)
    down = jnp.clip(down, 0, ns - 1)
    up = jnp.clip(up, 0, ns - 1)
    halos = (halo1, halo2)
    early = nchunk // 2

    def row_of(j):
        return j * sign + 3 * (1 - positive)

    def load_in(i):
        rows = pl.ds(pl.multiple_of(i * 4 * CHUNK, 4 * CHUNK), 4 * CHUNK)
        return pltpu.make_async_copy(x_ref.at[rows], stage.at[rows], in_sem.at[i])

    def halo_down(step, src, i):
        rows = pl.ds(pl.multiple_of(i * CHUNK, CHUNK), CHUNK)
        return pltpu.make_async_remote_copy(
            src_ref=src.at[pl.ds(2, 2), rows], dst_ref=halos[step].at[pl.ds(0, 2), rows],
            send_sem=hs_down.at[step, i], recv_sem=hr_up.at[step, i],
            device_id={"space": down}, device_id_type=MESH)

    def halo_up(step, src, i):
        rows = pl.ds(pl.multiple_of(i * CHUNK, CHUNK), CHUNK)
        return pltpu.make_async_remote_copy(
            src_ref=src.at[pl.ds(0, 1), rows], dst_ref=halos[step].at[pl.ds(2, 1), rows],
            send_sem=hs_up.at[step, i], recv_sem=hr_down.at[step, i],
            device_id={"space": up}, device_id_type=MESH)

    def send_halo(step, src, i):
        @pl.when(has_down)
        def _():
            halo_down(step, src, i).start()

        @pl.when(has_up)
        def _():
            halo_up(step, src, i).start()

    def wait_halo(step, src, i):
        @pl.when(has_up)
        def _():
            halo_down(step, src, i).wait_recv()

        @pl.when(has_down)
        def _():
            halo_up(step, src, i).wait_recv()

    def wait_sent(step, src, i):
        @pl.when(has_down)
        def _():
            halo_down(step, src, i).wait_send()

        @pl.when(has_up)
        def _():
            halo_up(step, src, i).wait_send()

    pl.loop(0, nchunk)(lambda i: load_in(i).start())

    barrier = pltpu.get_barrier_semaphore()
    for k in range(1, nv):
        pl.semaphore_signal(barrier, inc=1, device_id={"vel": lax.rem(me_v + k, nv)}, device_id_type=MESH)

    @pl.when(has_down)
    def _():
        pl.semaphore_signal(barrier, inc=1, device_id={"space": down}, device_id_type=MESH)

    @pl.when(has_up)
    def _():
        pl.semaphore_signal(barrier, inc=1, device_id={"space": up}, device_id_type=MESH)

    @pl.when(jnp.logical_not(has_up))
    def _():
        def fill(i):
            for halo in halos:
                for n in range(2):
                    halo[n, pl.ds(pl.multiple_of(i * 32, 32), 32), :] = jnp.zeros((32, LANES), jnp.float32)
        pl.loop(0, nchunk * CHUNK // 32)(fill)
        near[0] = jnp.zeros((16, LANES), jnp.float32)
        near[1] = jnp.zeros((16, LANES), jnp.float32)

    @pl.when(jnp.logical_not(has_down))
    def _():
        def fill(i):
            for halo in halos:
                halo[2, pl.ds(pl.multiple_of(i * 32, 32), 32), :] = jnp.zeros((32, LANES), jnp.float32)
        pl.loop(0, nchunk * CHUNK // 32)(fill)
        near[2] = jnp.zeros((16, LANES), jnp.float32)

    pl.semaphore_wait(barrier, nv - 1 + jnp.where(has_down, 1, 0) + jnp.where(has_up, 1, 0))

    def spread(i):
        load_in(i).wait()

        def tile(n):
            for m in range(4):
                v = pl.multiple_of(i * CHUNK + n * 32, 32) + 8 * m
                for j in range(4):
                    first[j, pl.ds(v, 8), :] = stage[pl.ds(v * 4 + row_of(j), 8, stride=4), :]
        pl.loop(0, CHUNK // 32)(tile)
        send_halo(0, first, i)
    pl.loop(0, nchunk)(spread)

    sub = lax.broadcasted_iota(jnp.int32, (8, LANES), 0)
    lane = lax.broadcasted_iota(jnp.int32, (8, LANES), 1)

    def clear():
        for k in range(13):
            for j in range(4):
                acc[k, j] = jnp.zeros((8, LANES), jnp.float32)

    def speed(index):
        return -LIMIT + SPACING * index.astype(jnp.float32)

    def move(i, src, halo, dst, collided):
        chunk = me_v * nchunk + i
        half = lax.rem(chunk, 2)
        x1 = speed(chunk // 2)
        cx = COURANT * jnp.abs(x1)
        ckx = cx * 0.5 * (1.0 - cx)
        up_shift = jnp.where(half == 1, 1, LANES - 1)
        down_shift = LANES - up_shift
        up_lane = jnp.where(half == 1, 0, LANES - 1)
        up_edge = lane == up_lane
        down_edge = lane == LANES - 1 - up_lane
        base = i * CHUNK
        for e in range(NVX // 8):
            def one(b, sums):
                v = pl.ds(pl.multiple_of(base + b * NVX + 8 * e, 8), 8)
                x2 = speed(half * HALF + b)
                cy = COURANT * jnp.abs(x2)
                cky = cy * 0.5 * (1.0 - cy)
                g = [halo[0, v, :], halo[1, v, :]] + [src[j, v, :] for j in range(4)] + [halo[2, v, :]]
                if collided:
                    g = [collide(g[n], n, b, e) for n in range(7)]
                g = sweep_rows(g, cx, ckx)
                new = []
                for j in range(4):
                    o = sweep_lanes(g[j], cy, cky, up_shift, down_shift, up_edge, down_edge)
                    dst[j, v, :] = o
                    s0, s1, s2, s3 = sums[4 * j : 4 * j + 4]
                    o1 = x2 * o
                    o2 = x2 * o1
                    new += [s0 + o, s1 + o1, s2 + o2, s3 + x2 * o2]
                return tuple(new)

            def several(n, sums):
                for m in range(UNROLL):
                    sums = one(n * UNROLL + m, sums)
                return sums

            sums = lax.fori_loop(0, HALF // UNROLL, several, (jnp.zeros((8, LANES), jnp.float32),) * 16)
            x3 = speed(sub + 8 * e)
            for j in range(4):
                s0, s1, s2, s3 = sums[4 * j : 4 * j + 4]
                t1 = x1 * s0
                t3 = x3 * s0
                t11 = x1 * t1
                t33 = x3 * t3
                whole = t11 + s2 + t33
                terms = [s0, t1, s1, t3, t11, s2, t33, x1 * s1, x1 * t3, x3 * s1,
                         x1 * whole, (x1 * x1 + x3 * x3) * s1 + s3, x3 * whole]
                for k in range(13):
                    acc[k, j] = acc[k, j] + terms[k]

    def reduce(step):
        for j in range(4):
            rows = [jnp.sum(acc[k, j], axis=0, keepdims=True) for k in range(13)]
            mom[step, row_of(j)] = jnp.concatenate(rows + [jnp.zeros((3, LANES), jnp.float32)], axis=0)
        mine = me_v // group

        def part(k):
            to = lax.rem(me_v + k, nv)
            return pltpu.make_async_remote_copy(
                src_ref=mom.at[step, to // group], dst_ref=gathered.at[step, me_v],
                send_sem=rs_send.at[step, k], recv_sem=rs_recv.at[step, me_v],
                device_id={"vel": to}, device_id_type=MESH)

        def part_in(k):
            frm = lax.rem(me_v + k, nv)
            return pltpu.make_async_remote_copy(
                src_ref=mom.at[step, 0], dst_ref=gathered.at[step, frm],
                send_sem=rs_send.at[step, k], recv_sem=rs_recv.at[step, frm],
                device_id={"vel": frm}, device_id_type=MESH)

        for k in range(1, nv):
            part(k).start()
        gathered[step, me_v] = mom[step, mine]
        for k in range(1, nv):
            part_in(k).wait_recv()
        total = gathered[step, 0]
        for n in range(1, nv):
            total = total + gathered[step, n]
        par[step, mine] = cell_parameters(total, kind_ref[pl.ds(mine, 1), :])

        def share(k):
            to = lax.rem(mine + k, 4) * group + lax.rem(me_v, group)
            return pltpu.make_async_remote_copy(
                src_ref=par.at[step, mine], dst_ref=par.at[step, mine],
                send_sem=ag_send.at[step, k], recv_sem=ag_recv.at[step, mine],
                device_id={"vel": to}, device_id_type=MESH)

        def share_in(k):
            row = lax.rem(mine + k, 4)
            return pltpu.make_async_remote_copy(
                src_ref=par.at[step, mine], dst_ref=par.at[step, row],
                send_sem=ag_send.at[step, k], recv_sem=ag_recv.at[step, row],
                device_id={"vel": row * group + lax.rem(me_v, group)}, device_id_type=MESH)

        for k in range(1, 4):
            share(k).start()
        for k in range(1, 4):
            share_in(k).wait_recv()
        for k in range(1, nv):
            part(k).wait_send()
        for k in range(1, 4):
            share(k).wait_send()

    def near_copy(n):
        j, to = ((2, down), (3, down), (0, up))[n]
        return pltpu.make_async_remote_copy(
            src_ref=par.at[0, row_of(j)], dst_ref=near.at[n],
            send_sem=np_send.at[n], recv_sem=np_recv.at[n],
            device_id={"space": to}, device_id_type=MESH)

    def parameters(step, n):
        if n in (0, 1):
            return near[n]
        if n == 6:
            return near[2]
        return par[step, row_of(n - 2)]

    def build_e(step, rows):
        x3 = speed(lax.broadcasted_iota(jnp.int32, (NVX, LANES), 0))
        for n in rows:
            p = parameters(step, n)
            c3 = x3 - p[2:3]
            quad = c3 * c3 * p[3:4]
            tab_e[0, n] = quad
            tab_e[1, n] = p[6:7] * c3
            tab_e[2, n] = jnp.exp(-0.5 * quad)
            tab_o[n] = jnp.broadcast_to(p[8:9], (8, LANES))

    def build_b(step, i, rows):
        chunk = me_v * nchunk + i
        x1 = speed(chunk // 2)
        x2 = speed(lax.rem(chunk, 2) * HALF + lax.broadcasted_iota(jnp.int32, (16, LANES), 0))
        for n in rows:
            p = parameters(step, n)
            c1 = x1 - p[0:1]
            c2 = x2 - p[1:2]
            quad = (c1 * c1 + c2 * c2) * p[3:4]
            tab_b[0, n] = quad - 5.0
            tab_b[1, n] = p[4:5] * c1 + p[5:6] * c2
            tab_b[2, n] = p[7:8] * jnp.exp(-0.5 * quad)

    def collide(f, n, b, e):
        es = pl.ds(8 * e, 8)
        bs = pl.ds(b, 1)
        quad = tab_b[0, n, bs, :] + tab_e[0, n, es, :]
        flow = tab_b[1, n, bs, :] + tab_e[1, n, es, :]
        gauss = tab_b[2, n, bs, :] * tab_e[2, n, es, :]
        return tab_o[n] * f + gauss * (1.0 + flow * quad)

    clear()

    def step_one(i):
        wait_halo(0, first, i)
        move(i, first, halo1, second, False)

        @pl.when(i < early)
        def _():
            send_halo(1, second, i)
    pl.loop(0, nchunk)(step_one)
    reduce(0)

    @pl.when(has_down)
    def _():
        near_copy(0).start()
        near_copy(1).start()

    @pl.when(has_up)
    def _():
        near_copy(2).start()
    pl.loop(early, nchunk)(lambda i: send_halo(1, second, i))
    clear()

    @pl.when(has_up)
    def _():
        near_copy(0).wait_recv()
        near_copy(1).wait_recv()

    @pl.when(has_down)
    def _():
        near_copy(2).wait_recv()

    build_e(0, range(7))

    def step_two(i):
        build_b(0, i, range(7))
        wait_halo(1, second, i)
        move(i, second, halo2, third, True)
    pl.loop(0, nchunk)(step_two)
    reduce(1)

    own = range(2, 6)
    build_e(1, own)

    def finish(i):
        build_b(1, i, own)
        for e in range(NVX // 8):
            def one(n):
                for m in range(UNROLL):
                    b = n * UNROLL + m
                    v = pl.multiple_of(i * CHUNK + b * NVX + 8 * e, 8)
                    for j in range(4):
                        out_ref[pl.ds(v * 4 + row_of(j), 8, stride=4), :] = collide(
                            third[j, pl.ds(v, 8), :], j + 2, b, e)
            pl.loop(0, HALF // UNROLL)(one)
    pl.loop(0, nchunk)(finish)

    for r in range(4):
        level_ref[r : r + 1, :] = par[1, r, 9:10, :]

    def drain(i):
        wait_sent(0, first, i)
        wait_sent(1, second, i)
    pl.loop(0, nchunk)(drain)

    @pl.when(has_down)
    def _():
        near_copy(0).wait_send()
        near_copy(1).wait_send()

    @pl.when(has_up)
    def _():
        near_copy(2).wait_send()


def per_device(nv, ns, initial, site_kind):
    amount, rows, lanes = initial.shape
    assert rows == 4 and lanes == LANES and amount % CHUNK == 0
    assert nv % 4 == 0 and (NVX * NVX * HALF) % amount == 0
    nchunk = amount // CHUNK
    f32 = jnp.float32
    dma = pltpu.SemaphoreType.DMA
    out, level = pl.pallas_call(
        functools.partial(kernel, nv, ns, nchunk),
        out_shape=(
            jax.ShapeDtypeStruct((amount * 4, LANES), f32),
            jax.ShapeDtypeStruct((4, LANES), f32),
        ),
        in_specs=[pl.BlockSpec(memory_space=pl.ANY), pl.BlockSpec(memory_space=pltpu.VMEM)],
        out_specs=(pl.BlockSpec(memory_space=pltpu.VMEM), pl.BlockSpec(memory_space=pltpu.VMEM)),
        scratch_shapes=[
            pltpu.VMEM((amount * 4, LANES), f32),
            pltpu.VMEM((4, amount, LANES), f32),
            pltpu.VMEM((4, amount, LANES), f32),
            pltpu.VMEM((4, amount, LANES), f32),
            pltpu.VMEM((3, amount, LANES), f32),
            pltpu.VMEM((3, amount, LANES), f32),
            pltpu.VMEM((13, 4, 8, LANES), f32),
            pltpu.VMEM((2, 4, 16, LANES), f32),
            pltpu.VMEM((2, nv, 16, LANES), f32),
            pltpu.VMEM((2, 4, 16, LANES), f32),
            pltpu.VMEM((3, 16, LANES), f32),
            pltpu.VMEM((3, 7, NVX, LANES), f32),
            pltpu.VMEM((7, 8, LANES), f32),
            pltpu.VMEM((3, 7, 16, LANES), f32),
            dma((nchunk,)),
            dma((2, nchunk)), dma((2, nchunk)), dma((2, nchunk)), dma((2, nchunk)),
            dma((2, nv)), dma((2, nv)), dma((2, 4)), dma((2, 4)), dma((3,)), dma((3,)),
        ],
        compiler_params=pltpu.CompilerParams(
            collective_id=0, has_side_effects=True, vmem_limit_bytes=50 * 1024 * 1024
        ),
    )(initial.reshape(amount * 4, LANES), site_kind)
    return out.reshape(amount, 4, LANES), level


def solution(mesh):
    return jax.shard_map(
        functools.partial(per_device, mesh.shape["vel"], mesh.shape["space"]),
        mesh=mesh,
        in_specs=(P("vel", "space", None), P("space", None)),
        out_specs=(P("vel", "space", None), P("space", None)),
        check_vma=False,
    )
```
